512 devices in a mesh: section: 32 (over z, x_lo), tensor: 16 (over y, x_hi, core).
Axes of the slice: x: 4 (x_hi: 2, x_lo: 2; x = x_hi * 2 + x_lo), y: 4, z: 16, core: 2. Of those that a mesh axis runs over, the one named last changes fastest.
Arguments:
- old_query: bfloat16 [32, 4096, 4096], P('section', 'tensor'), may hold values from -0.09375 to 0.09375
- old_key: bfloat16 [32, 4096, 1024], P('section', 'tensor'), may hold values from -0.09375 to 0.09375
- old_value: bfloat16 [32, 4096, 1024], P('section', 'tensor'), may hold values from -0.09375 to 0.09375
- depth_mix: float32 [32], replicated, may hold values from -1 to 1
- width_query: bfloat16 [8192, 4096], P('section', 'tensor'), may hold values from -0.09375 to 0.09375
- width_kv: bfloat16 [1024, 1024], P('section', 'tensor'), may hold values from -0.1875 to 0.1875
- width_stream: bfloat16 [8192, 4096], P('tensor', 'section'), may hold values from -0.0625 to 0.0625
- hidden: bfloat16 [2048, 8192], P('section', 'tensor'), may hold values from -8 to 8
Outputs:
- grown_query: bfloat16 [8192, 8192], P('tensor', 'section')
- grown_key: bfloat16 [8192, 1024], P('tensor', 'section')
- grown_value: bfloat16 [8192, 1024], P('tensor', 'section')
- attended: bfloat16 [2048, 8192], P('tensor', 'section')
The draws below stay inside these ranges and needn't reach their ends.
All inputs are finite; a program needn't handle non-finite values.
Results may differ from the reference program's by a relative error of at most 0.034.
Values may be sent and summed in bfloat16 or wider, within the bound.
No kernel may reach another device: no remote copies, remote signals or barrier semaphores. Data moves between devices by JAX's collectives and lax.ppermute only.
A program may use at most 64 MiB of HBM per device.

```python
import math
import jax
import jax.numpy as jnp
from jax import lax

D1 = 4096
D2 = 8192
HEADS = 64
HD = 128
KVH = 8
KVW = 1024
OLD = 32
SEQ_LEN = 2048


def draw_hidden(key, part):
    key = jax.random.fold_in(key, 11)
    base_key = jax.random.fold_in(key, 0)
    return jnp.clip(jax.random.normal(base_key, (SEQ_LEN, D2), jnp.float32), -4.0, 4.0).astype(jnp.bfloat16)


def level_of(key, extent, shards, least, top_value):
    def one(dim, blocks):
        steps = jax.random.uniform(jax.random.fold_in(jax.random.fold_in(key, 6), dim), (blocks,), jnp.float32, least / len(shards), top_value / len(shards))
        return jnp.repeat(jnp.exp(steps), extent[dim] // blocks).reshape((-1,) + (1,) * (len(extent) - dim - 1))

    factor_of = one(*shards[0])
    for cut in shards[1:]:
        factor_of = factor_of * one(*cut)
    return factor_of


def bell_draw(own_key, shape, deviation, limit, cuts=(), held_as=jnp.bfloat16):
    factor_of = level_of(own_key, shape, cuts, -0.22, 0.18) if cuts else 1.0
    array = jax.random.normal(own_key, shape, jnp.float32) * deviation * factor_of
    return jnp.minimum(jnp.maximum(array, -limit), limit).astype(held_as)


def setup_inputs(seed: int = 0) -> dict:
    key_of = jax.random.split(jax.random.key(seed), 9)
    old_query = bell_draw(key_of[0], (OLD, D1, D1), D1 ** -0.5, 0.09375, ((0, 32), (1, 16)))
    old_key = bell_draw(key_of[1], (OLD, D1, KVW), D1 ** -0.5, 0.09375, ((0, 32), (1, 16)))
    old_value = bell_draw(key_of[2], (OLD, D1, KVW), D1 ** -0.5, 0.09375, ((0, 32), (1, 16)))
    depth_mix = bell_draw(key_of[3], (OLD,), OLD ** -0.5, 1.0, (), jnp.float32)
    width_query = bell_draw(key_of[4], (D2, D1), D1 ** -0.5, 0.09375, ((0, 32), (1, 16)))
    width_kv = bell_draw(key_of[5], (KVW, KVW), KVW ** -0.5, 0.1875, ((0, 32), (1, 16)))
    width_stream = bell_draw(key_of[6], (D2, D1), D2 ** -0.5, 0.0625, ((0, 16), (1, 32)))
    hidden = draw_hidden(jax.random.fold_in(key_of[8], 71), 0)
    return dict(old_query=old_query, old_key=old_key, old_value=old_value, depth_mix=depth_mix, width_query=width_query, width_kv=width_kv, width_stream=width_stream, hidden=hidden)


def mix_layers(depth_mix, stacked):

    def add_layer(layer_index, running):
        return running + depth_mix[layer_index] * stacked[layer_index].astype(jnp.float32)
    initial = jnp.zeros(stacked.shape[1:], jnp.float32)
    return lax.fori_loop(0, stacked.shape[0], add_layer, initial).astype(jnp.bfloat16)

def contract_last(left_side, right_side):
    return lax.dot_general(left_side.astype(jnp.float32), right_side.astype(jnp.float32), (((1,), (1,)), ((), ())), preferred_element_type=jnp.float32)

def product(left_side, right_side):
    return jnp.dot(left_side.astype(jnp.float32), right_side.astype(jnp.float32), preferred_element_type=jnp.float32)

def reference(old_query, old_key, old_value, depth_mix, width_query, width_kv, width_stream, hidden):
    mixed_query = mix_layers(depth_mix, old_query)
    mixed_key = mix_layers(depth_mix, old_key)
    mixed_value = mix_layers(depth_mix, old_value)
    expanded_query = contract_last(mixed_query, width_query).astype(jnp.bfloat16)
    expanded_key = contract_last(mixed_key, width_kv).astype(jnp.bfloat16)
    expanded_value = contract_last(mixed_value, width_kv).astype(jnp.bfloat16)
    grown_query = product(width_stream, expanded_query).astype(jnp.bfloat16)
    grown_key = product(width_stream, expanded_key).astype(jnp.bfloat16)
    grown_value = product(width_stream, expanded_value).astype(jnp.bfloat16)
    joined = jnp.concatenate([grown_query, grown_key, grown_value], axis=1)
    projections = product(hidden, joined)
    queries = projections[:, :D2].astype(jnp.bfloat16)
    key_rows = projections[:, D2:D2 + KVW].astype(jnp.bfloat16)
    value_rows = projections[:, D2 + KVW:].astype(jnp.bfloat16)
    score_scale = 1.0 / math.sqrt(HD)
    positions = jnp.arange(SEQ_LEN, dtype=jnp.int32)
    causal = positions[None, :] <= positions[:, None]
    query_heads = queries.reshape(SEQ_LEN, HEADS, HD).transpose(1, 0, 2)
    key_heads = key_rows.reshape(SEQ_LEN, KVH, HD).transpose(1, 0, 2)
    value_heads = value_rows.reshape(SEQ_LEN, KVH, HD).transpose(1, 0, 2)

    def one_head(head_index):
        head_query = query_heads[head_index]
        head_key = key_heads[head_index % KVH]
        head_value = value_heads[head_index % KVH]
        scores = lax.dot_general(head_query, head_key, (((1,), (1,)), ((), ())), preferred_element_type=jnp.float32) * score_scale
        scores = jnp.where(causal, scores, -jnp.inf)
        row_max = lax.optimization_barrier(jnp.max(scores, axis=1, keepdims=True))
        weights = jnp.exp(scores - row_max)
        denominator = lax.optimization_barrier(jnp.sum(weights, axis=1, keepdims=True))
        probs = weights.astype(jnp.bfloat16)
        output = jnp.dot(probs, head_value, preferred_element_type=jnp.float32) / denominator
        return output.astype(jnp.bfloat16)
    heads_out = lax.map(one_head, jnp.arange(HEADS, dtype=jnp.int32))
    attended = heads_out.transpose(1, 0, 2).reshape(SEQ_LEN, D2)
    return (grown_query, grown_key, grown_value, attended)
```

```python
import math

import jax
import jax.numpy as jnp
from jax import lax
from jax.experimental import pallas as pl
from jax.experimental.pallas import tpu as pltpu
from jax.sharding import Mesh, PartitionSpec as P

HD = 128
KVH = 8
BF = jnp.bfloat16
F32 = jnp.float32
Z = ("q", "r")
SECTION = ("q", "r", "x")
TENSOR = ("y", "h", "c")
Q, R, X, Y, H, C = 4, 4, 2, 4, 2, 2
ZS, TS = Q * R, Y * H * C


def shift(value, distance):
    return lax.ppermute(value, Z, [(i, (i + distance) % ZS) for i in range(ZS)])


def partner(value, axis, bit=1):
    size = {"x": X, "y": Y, "h": H, "c": C, "r": R}[axis]
    return lax.ppermute(value, axis, [(i, i ^ bit) for i in range(size)])


def pair_up(value, axis, dim, bit=1):
    other = partner(value, axis, bit)
    low = (lax.axis_index(axis) & bit) == 0
    return jnp.concatenate([jnp.where(low, value, other), jnp.where(low, other, value)], axis=dim)


def gather_tensor(value):
    shape = value.shape
    value = pair_up(value[None], "h", 0)
    value = pair_up(value[None], "y", 0, 1)
    value = pair_up(value[None], "y", 0, 2)
    value = pair_up(value.reshape((Y * H, 1) + shape), "c", 1)
    return value.reshape((TS,) + shape)


def gather_blocks(value):
    for axis, bit in (("h", 1), ("y", 1), ("y", 2)):
        value = jnp.stack([value, partner(value, axis, bit)], axis=0)
    shape = value.shape[3:]
    value = value.reshape((Y * H,) + shape)
    return value, partner(value, "c")


def dot(a, b, ca, cb):
    return lax.dot_general(a, b, (((ca,), (cb,)), ((), ())), preferred_element_type=F32)


def in_vmem(count):
    return [pl.BlockSpec(memory_space=pltpu.SMEM)] + [pl.BlockSpec(memory_space=pltpu.VMEM)] * count


def expand_query(index, mixed, own, other, n_q, gap):
    rows = mixed.shape[0]
    count, _, part = own.shape

    def kernel(index_ref, mixed_ref, own_ref, other_ref, out_ref):
        t = index_ref[0]
        low = jnp.zeros((rows, n_q), F32)
        high = jnp.zeros((rows, n_q), F32)
        for i in range(count):
            for bit, ref in ((0, own_ref), (1, other_ref)):
                chunk = t ^ (2 * i + bit)
                left = mixed_ref[:, pl.ds(pl.multiple_of(chunk * part, part), part)]
                low += dot(left, ref[i, :n_q, :], 1, 1)
                high += dot(left, ref[i, gap : gap + n_q, :], 1, 1)
        out_ref[:, :n_q] = low.astype(BF)
        out_ref[:, n_q:] = high.astype(BF)

    return pl.pallas_call(
        kernel,
        out_shape=jax.ShapeDtypeStruct((rows, 2 * n_q), BF),
        in_specs=in_vmem(3),
        out_specs=pl.BlockSpec(memory_space=pltpu.VMEM),
        compiler_params=pltpu.CompilerParams(vmem_limit_bytes=24 << 20),
        cost_estimate=pl.CostEstimate(
            flops=4 * rows * n_q * 2 * count * part,
            bytes_accessed=2 * (mixed.size + own.size + other.size + 2 * rows * n_q),
            transcendentals=0,
        ),
    )(index, mixed, own, other)


def attend(index, queries, own, other):
    rows, width = queries.shape
    heads, count = width // HD, own.shape[0]
    tokens = own.shape[2]
    scale = 1.0 / math.sqrt(HD)
    blocks = [(i, bit) for i in range(count) for bit in (0, 1)]

    def kernel(index_ref, query_ref, own_ref, other_ref, out_ref, scores_ref):
        t = index_ref[0]
        refs = (own_ref, other_ref)
        query_position = t * rows + lax.broadcasted_iota(jnp.int32, (rows, tokens), 0)
        key_offset = lax.broadcasted_iota(jnp.int32, (rows, tokens), 1)
        for head in range(heads):
            at = head * HD
            query = query_ref[:, at : at + HD]
            for n, (i, bit) in enumerate(blocks):
                block = t ^ (2 * i + bit)
                value = dot(query, refs[bit][i, at : at + HD, :], 1, 0) * scale
                seen = block * tokens + key_offset <= query_position
                scores_ref[:, n * tokens : (n + 1) * tokens] = jnp.where(seen, value, -jnp.inf)
            row_max = jnp.max(scores_ref[...], axis=1, keepdims=True)
            denominator = jnp.zeros((rows, 1), F32)
            total = jnp.zeros((rows, HD), F32)
            for n, (i, bit) in enumerate(blocks):
                weights = jnp.exp(scores_ref[:, n * tokens : (n + 1) * tokens] - row_max)
                denominator += jnp.sum(weights, axis=1, keepdims=True)
                value_head = refs[bit][i, width + at : width + at + HD, :]
                total += dot(weights.astype(BF), value_head, 1, 1)
            out_ref[:, at : at + HD] = (total / denominator).astype(BF)

    return pl.pallas_call(
        kernel,
        out_shape=jax.ShapeDtypeStruct((rows, width), BF),
        in_specs=in_vmem(3),
        out_specs=pl.BlockSpec(memory_space=pltpu.VMEM),
        scratch_shapes=[pltpu.VMEM((rows, 2 * count * tokens), F32)],
        compiler_params=pltpu.CompilerParams(vmem_limit_bytes=24 << 20),
        cost_estimate=pl.CostEstimate(
            flops=8 * rows * width * count * tokens,
            bytes_accessed=2 * (own.size + other.size + 2 * rows * width),
            transcendentals=2 * rows * heads * count * tokens,
        ),
    )(index, queries, own, other)


def per_device(
    old_query, old_key, old_value, depth_mix, width_query, width_kv, width_stream, hidden
):
    z = lax.axis_index(Z)
    x = lax.axis_index("x")
    t = lax.axis_index(TENSOR)
    index = t[None].astype(jnp.int32)

    stream = lax.all_gather(width_stream, Z, axis=1, tiled=True)

    old = jnp.concatenate([old_query[0], old_key[0], old_value[0]], axis=1)
    rows, cols = old.shape[0] // X, old.shape[1]
    half = cols // 2
    deep = rows // ZS
    blocks = old.reshape(X, Q, R, deep, cols)

    def weight(offset):
        return lax.dynamic_index_in_dim(depth_mix, ((z + offset) % ZS) * X + x, 0, False)

    def for_class(offset):
        return lax.dynamic_index_in_dim(blocks, (z + offset) % R, 2, False)

    after, before, far, width_query = lax.optimization_barrier(
        (for_class(1), for_class(3), for_class(2), width_query)
    )
    after, before = shift(after, 1), shift(before, -1)
    far_low, far_high = shift(far[..., :half], 2), shift(far[..., half:], -2)
    close = (
        for_class(0).astype(F32) * weight(0)
        + after.astype(F32) * weight(-1)
        + before.astype(F32) * weight(1)
    )
    summed_near = jnp.concatenate(
        [
            close[..., :half] + far_low.astype(F32) * weight(-2),
            close[..., half:] + far_high.astype(F32) * weight(2),
        ],
        axis=-1,
    ).astype(BF)
    keep = lax.dynamic_index_in_dim(summed_near, x, 0, False)
    other = partner(lax.dynamic_index_in_dim(summed_near, 1 - x, 0, False), "x")
    summed = (keep.astype(F32) + other.astype(F32)).astype(BF)
    pieces = lax.all_to_all(summed, "q", 0, 0, tiled=True)
    pieces, stream = lax.optimization_barrier((pieces, stream))
    mixed_rows = jnp.sum(pieces.astype(F32), axis=0).astype(BF)

    kv_rows, kv_part = width_kv.shape
    n_q, part = width_query.shape
    flat_kv = width_kv.reshape(kv_rows * kv_part // part, part)
    n_kv = flat_kv.shape[0]
    widths = jnp.concatenate([width_query, flat_kv, jnp.zeros_like(flat_kv)], axis=0)
    gap = widths.shape[0]
    widths = jnp.concatenate([widths, partner(widths, "x")], axis=0)
    width_own, width_other = gather_blocks(widths)

    def unflatten(start):
        own = width_own[:, start : start + n_kv]
        other = width_other[:, start : start + n_kv]
        by_distance = jnp.stack([own, other], axis=1).reshape((TS,) + own.shape[1:])
        rows = jnp.take(by_distance, t ^ jnp.arange(TS), axis=0)
        return (
            rows.reshape(TS, n_kv, kv_rows // n_kv, kv_part)
            .transpose(1, 2, 0, 3)
            .reshape(kv_rows, TS * kv_part)
        )

    wide_kv = jnp.concatenate([unflatten(0 + n_q), unflatten(gap + n_q)], axis=0)

    tokens = pair_up(hidden, "x", 0)
    token_rows = tokens.shape[0]
    streamed = dot(tokens, stream, 1, 0).astype(BF)
    streamed = streamed.reshape(token_rows, TS, -1).transpose(1, 0, 2)
    streamed = lax.all_to_all(streamed, TENSOR, 0, 0, tiled=True)
    streamed = jnp.sum(streamed.astype(F32), axis=0)
    rounded = lax.reduce_precision(streamed, 8, 7)
    streamed = jnp.concatenate([rounded, streamed - rounded], axis=0).astype(BF)
    turn = [
        ((zz * X + xx) * TS + tt, (tt * X + xx) * TS + zz)
        for zz in range(ZS)
        for xx in range(X)
        for tt in range(TS)
    ]
    streamed = lax.ppermute(streamed, SECTION + TENSOR, turn)

    near = lax.all_to_all(
        jnp.broadcast_to(mixed_rows[None], (Q,) + mixed_rows.shape), "q", 0, 0, tiled=True
    )
    of_after, of_before = shift(near, -1), shift(near, 1)
    of_far = jnp.concatenate([shift(near[..., :half], 2), shift(near[..., half:], -2)], axis=2)
    mixed = jnp.stack([near, of_after, of_far, of_before], axis=0).reshape(rows, cols)
    mixed, streamed = lax.optimization_barrier((mixed, streamed))
    streamed = lax.all_gather(streamed, Z, axis=1, tiled=True)

    wide_in, kv_in = TS * part, TS * kv_part
    expanded_query = expand_query(index, mixed, width_own, width_other, n_q, gap)
    expanded_key = dot(mixed[:, wide_in : wide_in + kv_in], wide_kv, 1, 1).astype(BF)
    expanded_value = dot(mixed[:, wide_in + kv_in :], wide_kv, 1, 1).astype(BF)
    expanded = jnp.concatenate(
        [
            expanded_query,
            expanded_key[:, :kv_rows],
            expanded_value[:, :kv_rows],
            expanded_key[:, kv_rows:],
            expanded_value[:, kv_rows:],
        ],
        axis=1,
    )
    width = expanded.shape[1]
    blocks = expanded.reshape(R, Q, deep, width)
    blocks = lax.dynamic_slice_in_dim(jnp.concatenate([blocks, blocks], 0), (R - z % R) % R, R, 0)
    expanded = blocks.transpose(1, 0, 2, 3).reshape(rows, width)
    whole = gather_tensor(expanded).reshape(TS * rows, width)

    grown_rows = stream.shape[0]
    whole_query, whole_kv = whole[:, : 2 * n_q], whole[:, 2 * n_q :]
    by_kv = dot(whole_kv, streamed, 0, 1)
    by_kv = jnp.concatenate(
        [dot(whole_kv, stream, 0, 1), by_kv[:, :token_rows] + by_kv[:, token_rows:]], axis=1
    )
    by_query = dot(streamed, whole_query, 1, 0)
    by_query = jnp.concatenate(
        [dot(stream, whole_query, 1, 0), by_query[:token_rows] + by_query[token_rows:]], axis=0
    )
    n_mine = 2 * kv_rows
    other_kv = partner(
        jnp.concatenate([by_kv[n_mine:], by_kv[:n_mine, grown_rows:]], axis=1).astype(BF), "x"
    ).astype(F32)
    other_query = partner(by_query[:, n_q:].astype(BF), "x")
    full_query = (by_query[:, :n_q] + other_query.astype(F32)).astype(BF)
    full_kv = (by_kv[:n_mine] + other_kv[:, : by_kv.shape[1]]).astype(BF)
    its_kv = (by_kv[n_mine:, grown_rows:] + other_kv[:, by_kv.shape[1] :]).astype(BF)
    grown_key = full_kv[:kv_rows, :grown_rows].T
    grown_value = full_kv[kv_rows:, :grown_rows].T

    heads_here = n_q // HD
    kv_mine = full_kv[:, grown_rows:]
    pair = jnp.stack(
        [jnp.where(x == 0, kv_mine, its_kv), jnp.where(x == 0, its_kv, kv_mine)], axis=0
    )[None]
    pair = pair_up(pair, "r", 0, 1)
    pair = pair_up(pair, "r", 0, 2)
    heads_pair = pair.reshape(R * X, 2, kv_rows, token_rows).transpose(1, 0, 2, 3)
    heads_pair = heads_pair.reshape(2 * heads_here * HD, token_rows)
    heads_pair, full_query = lax.optimization_barrier((heads_pair, full_query))
    grown_query, queries = full_query[:grown_rows], full_query[grown_rows:]
    pairs = KVH // heads_here
    route = []
    for src in range(ZS * X):
        zz, xx = src // X, src % X
        route.append((src, ((zz % R) * X + xx) * pairs + zz // R))
    kv_own, kv_other = gather_blocks(lax.ppermute(heads_pair, SECTION, route))
    attended = attend(index, queries, kv_own, kv_other)
    return (grown_query, grown_key, grown_value, attended)


def solution(mesh):
    fine = Mesh(mesh.devices.reshape(Q, R, X, Y, H, C), SECTION + TENSOR)
    placed = (
        P(SECTION, TENSOR, None),
        P(SECTION, TENSOR, None),
        P(SECTION, TENSOR, None),
        P(),
        P(SECTION, TENSOR),
        P(SECTION, TENSOR),
        P(TENSOR, SECTION),
        P(SECTION, TENSOR),
    )
    return jax.shard_map(
        per_device,
        mesh=fine,
        in_specs=placed,
        out_specs=(P(TENSOR, SECTION),) * 4,
        check_vma=False,
    )
```
